512 devices in a mesh: grp: 32 (over y_hi, z, core), lane: 16 (over x, y_lo).
Axes of the slice: x: 4, y: 8 (y_hi: 2, y_lo: 4; y = y_hi * 4 + y_lo), z: 8, core: 2. Of those that a mesh axis runs over, the one named last changes fastest.
Arguments:
- passage_query: bfloat16 [32, 16, 3, 128, 2048], P('grp', 'lane'), may hold values from -6 to 6
- passage_keyval: bfloat16 [32, 16, 3, 2, 128, 1024], P('grp', 'lane'), may hold values from -12 to 12
- prefix_keys: bfloat16 [32, 1024, 1024], P('grp', 'lane'), may hold values from -16 to 16
- prefix_values: bfloat16 [32, 1024, 1024], P('grp', 'lane'), may hold values from -6 to 6
- home_count: int32 [32, 16], P('grp', 'lane'), may hold values from 1 to 3, as said below
- move_slot: int32 [32, 16], P('grp', 'lane'), may hold values from 0 to 3, as said below
- score_weight: bfloat16 [2048], replicated, may hold values from -0.125 to 0.125
Outputs:
- attended: bfloat16 [32, 16, 2, 128, 2048], P('grp', 'lane')
- scores: float32 [32, 16, 3], P('grp', 'lane')
The draws below stay inside these ranges and needn't reach their ends.
Inputs may be any that keep to these rules, and one draw needn't show every extreme that they name: Home slots 0 .. home_count - 1 of device (g, l) hold passages of query g; some device holds 3. `move_slot`: a live home slot of (g, l) whose passage runs on device (g+1 mod 32, l), or 3 for none; on every device the kept passages plus the one received are at most 2, and some device runs 2.
All inputs are finite; a program needn't handle non-finite values.
Results may differ from the reference program's by a relative error of at most 0.009.
Values may be sent and summed in bfloat16 or wider, within the bound.
A program may use at most 128 MiB of HBM per device.

```python
import math
import jax
import jax.numpy as jnp
from jax import lax

H = 8
KVH = 4
HD = 256
L = 128
P_SIZE = 1024
HS = 3
RS = 2
GROUPS = 32
LANES = 16


def balance_plan(key):
    key_flag, key_keep, key_slot, key_spot = jax.random.split(key, 4)
    spot_draw = jax.random.randint(key_spot, (2,), 0, 1 << 20)
    spot_group = spot_draw[0] % GROUPS
    spot_lane = spot_draw[1] % LANES
    group_ids = jnp.arange(GROUPS, dtype=jnp.int32)[:, None]
    lane_ids = jnp.arange(LANES, dtype=jnp.int32)[None, :]
    at_spot = (group_ids == spot_group) & (lane_ids == spot_lane)
    before_spot = (group_ids == (spot_group + GROUPS - 1) % GROUPS) & (lane_ids == spot_lane)
    moved_flag = jax.random.randint(key_flag, (GROUPS, LANES), 0, 2)
    moved_flag = jnp.where(at_spot, 1, jnp.where(before_spot, 0, moved_flag))
    received = jnp.roll(moved_flag, 1, axis=0)
    lowest = 1 - moved_flag
    highest = RS - received
    kept_count = lowest + jax.random.randint(key_keep, (GROUPS, LANES), 0, 1 << 20) % (highest - lowest + 1)
    kept_count = jnp.where(at_spot, RS, kept_count)
    live_count = kept_count + moved_flag
    chosen = jax.random.randint(key_slot, (GROUPS, LANES), 0, 1 << 20) % live_count
    move_index = jnp.where(moved_flag == 1, chosen, HS)
    return (live_count.astype(jnp.int32), move_index.astype(jnp.int32))


def draw_home_count(key, part):
    return balance_plan(key)[0]


def draw_move_slot(key, part):
    return balance_plan(key)[1]


def draw_prefix_keys(key, part):
    key = jax.random.fold_in(key, 7)
    key_base, key_rows, key_cols = jax.random.split(key, 3)
    shape = (GROUPS, P_SIZE, KVH * HD)
    row_scale = jnp.exp(jax.random.uniform(key_rows, (GROUPS, P_SIZE, 1), jnp.float32, math.log(0.8), math.log(1.25)))
    col_scale = jnp.exp(jax.random.uniform(key_cols, (1, 1, KVH * HD), jnp.float32, math.log(0.5), math.log(2.0)))
    base = jax.random.normal(key_base, shape, jnp.float32)
    return jnp.clip(base * row_scale * col_scale, -16.0, 16.0).astype(jnp.bfloat16)


def shard_levels(key, extent, cuts, least, largest):
    gain = 1.0
    for position, blocks in cuts:
        heights = jax.random.uniform(jax.random.fold_in(jax.random.fold_in(key, 6), position), (blocks,), jnp.float32, least / len(cuts), largest / len(cuts))
        gain = gain * jnp.repeat(jnp.exp(heights), extent[position] // blocks).reshape((-1,) + (1,) * (len(extent) - 1 - position))
    return gain


def bell_draw(own_key, dims, spread, most, cuts=(), kind=jnp.bfloat16):
    values = jax.random.normal(own_key, dims, jnp.float32) * spread
    if len(cuts) > 0:
        values = shard_levels(own_key, dims, cuts, -0.22, 0.18) * values
    return jnp.clip(values, min=-most, max=most).astype(kind)


def setup_inputs(seed: int = 0) -> dict:
    streams_of = jax.random.split(jax.random.key(seed), 8)
    passage_query = bell_draw(streams_of[0], (GROUPS, LANES, HS, L, H * HD), 1.0, 6.0, ((0, 32), (1, 16)))
    passage_keyval = bell_draw(streams_of[1], (GROUPS, LANES, HS, 2, L, KVH * HD), 2.0, 12.0, ((0, 32), (1, 16)))
    prefix_keys = draw_prefix_keys(jax.random.fold_in(streams_of[7], 71), 0)
    prefix_values = bell_draw(streams_of[3], (GROUPS, P_SIZE, KVH * HD), 1.0, 6.0, ((0, 32), (1, 16)))
    home_count = draw_home_count(jax.random.fold_in(streams_of[7], 71), 0)
    move_slot = draw_move_slot(jax.random.fold_in(streams_of[7], 71), 0)
    score_weight = bell_draw(streams_of[6], (H * HD,), (H * HD) ** -0.5, 0.125)
    return {"passage_query": passage_query, "passage_keyval": passage_keyval, "prefix_keys": prefix_keys, "prefix_values": prefix_values, "home_count": home_count, "move_slot": move_slot, "score_weight": score_weight}


softcap = 50.0


def run_tables(home_count, move_slot):
    moved_flag = (move_slot < HS).astype(jnp.int32)
    kept_count = home_count - moved_flag
    guest_flag = jnp.roll(moved_flag, 1, axis=0)
    run_index = jnp.arange(RS, dtype=jnp.int32)[None, None, :]
    own_source = run_index + (run_index >= move_slot[:, :, None]).astype(jnp.int32)
    is_own = run_index < kept_count[:, :, None]
    is_guest = (run_index == kept_count[:, :, None]) & (guest_flag[:, :, None] == 1)
    return kept_count, own_source, is_own, is_guest


def slot_attention(query_rows, keyval_rows, prefix_key, prefix_value):
    slot_count = query_rows.shape[0]
    group_size = H // KVH
    queries = query_rows.reshape(slot_count, L, KVH, group_size, HD).astype(jnp.float32)
    key_rows = jnp.concatenate([prefix_key, keyval_rows[:, 0]], axis=1)
    key_rows = key_rows.reshape(slot_count, P_SIZE + L, KVH, HD).astype(jnp.float32)
    value_rows = jnp.concatenate([prefix_value, keyval_rows[:, 1]], axis=1)
    value_rows = value_rows.reshape(slot_count, P_SIZE + L, KVH, HD).astype(jnp.float32)
    products = jnp.einsum("stgrd,sugd->sgrtu", queries, key_rows) * HD ** -0.5
    logits = softcap * jnp.tanh(products / softcap)
    allowed = jnp.arange(P_SIZE + L, dtype=jnp.int32)[None, :] <= P_SIZE + jnp.arange(L, dtype=jnp.int32)[:, None]
    exponent = jnp.where(allowed, jnp.exp(logits), jnp.zeros_like(logits))
    weights = lax.optimization_barrier(exponent.astype(jnp.bfloat16)).astype(jnp.float32)
    numerator = jnp.einsum("sgrtu,sugd->stgrd", weights, value_rows)
    denominator = jnp.transpose(jnp.sum(exponent, axis=-1), (0, 3, 1, 2))[..., None]
    return (numerator / denominator).reshape(slot_count, L, H * HD).astype(jnp.bfloat16)


def reference(passage_query, passage_keyval, prefix_keys, prefix_values, home_count, move_slot, score_weight):
    kept_count, own_source, is_own, is_guest = run_tables(home_count, move_slot)
    pick_slot = jnp.minimum(move_slot, HS - 1)
    row_width = H * HD

    def one_group(group):
        before = (group + GROUPS - 1) % GROUPS
        guest_query = jnp.take_along_axis(passage_query[before], pick_slot[before][:, None, None, None], axis=1)
        guest_keyval = jnp.take_along_axis(passage_keyval[before], pick_slot[before][:, None, None, None, None], axis=1)
        own_query = jnp.take_along_axis(passage_query[group], own_source[group][:, :, None, None], axis=1)
        own_keyval = jnp.take_along_axis(passage_keyval[group], own_source[group][:, :, None, None, None], axis=1)
        guest_mark = is_guest[group]
        run_query = jnp.where(guest_mark[:, :, None, None], guest_query, own_query)
        run_keyval = jnp.where(guest_mark[:, :, None, None, None], guest_keyval, own_keyval)
        flat_mark = guest_mark.reshape(LANES * RS, 1, 1)
        slot_keys = jnp.where(flat_mark, prefix_keys[before][None], prefix_keys[group][None])
        slot_values = jnp.where(flat_mark, prefix_values[before][None], prefix_values[group][None])
        result = slot_attention(run_query.reshape(LANES * RS, L, row_width),
                                run_keyval.reshape(LANES * RS, 2, L, KVH * HD), slot_keys, slot_values)
        result = result.reshape(LANES, RS, L, row_width)
        live = (is_own[group] | guest_mark)[:, :, None, None]
        return jnp.where(live, result, jnp.zeros_like(result))

    attended = lax.map(one_group, jnp.arange(GROUPS, dtype=jnp.int32))
    last_rows = attended[:, :, :, L - 1, :].reshape(GROUPS * LANES * RS, row_width)
    slot_score = jnp.dot(last_rows, score_weight, preferred_element_type=jnp.float32).reshape(GROUPS, LANES, RS)
    guest_score = jnp.take_along_axis(slot_score, jnp.minimum(kept_count, RS - 1)[:, :, None], axis=2)[:, :, 0]
    returned = jnp.roll(guest_score, -1, axis=0)
    home_index = jnp.arange(HS, dtype=jnp.int32)[None, None, :]
    run_place = jnp.clip(home_index - (home_index > move_slot[:, :, None]).astype(jnp.int32), 0, RS - 1)
    own_score = jnp.take_along_axis(slot_score, run_place, axis=2)
    zeros_home = jnp.zeros(own_score.shape, jnp.float32)
    scores = jnp.where(home_index == move_slot[:, :, None], returned[:, :, None],
                       jnp.where(home_index < home_count[:, :, None], own_score, zeros_home))
    return attended, scores
```

```python
import functools

import jax
import jax.numpy as jnp
from jax import lax
from jax.experimental import pallas as pl
from jax.experimental.pallas import tpu as pltpu
from jax.sharding import PartitionSpec as P

MESH = pl.DeviceIdType.MESH
HD = 256
KVH = 4
SIDE = 4
SOFTCAP = 50.0
NT = (((1,), (1,)), ((), ()))


def kernel(
    query_ref, keyval_ref, pkeys_ref, pvalues_ref, count_ref, move_ref, weight_ref,
    att_ref, score_ref,
    kbuf, vbuf, query, keyval, num, den, own, sent, guest, sums,
    load_sem, y_send, x_send, relay_send, y_recv, x_recv, relay_recv, g_send, g_recv,
):
    groups = lax.axis_size("grp")
    g = lax.axis_index("grp")
    lane = lax.axis_index("lane")
    x, y = lane // SIDE, lax.rem(lane, SIDE)
    tokens = query.shape[1]
    rows = pkeys_ref.shape[0]
    col = rows * SIDE
    bufs = (kbuf, vbuf)

    right = (g, lax.rem(x + 1, SIDE) * SIDE + y)
    left = (g, lax.rem(x + 3, SIDE) * SIDE + y)
    above = [(g, x * SIDE + lax.rem(y + d, SIDE)) for d in (1, 2, 3)]
    ahead = (lax.rem(g + 1, groups), lane)
    behind = (lax.rem(g + groups - 1, groups), lane)

    barrier = pltpu.get_barrier_semaphore()
    for other in (right, left, *above, ahead, behind):
        pl.semaphore_signal(barrier, inc=1, device_id=other, device_id_type=MESH)

    def block(xx, yy):
        return pl.ds(pl.multiple_of((xx * SIDE + yy) * rows, rows), rows)

    loads = []
    for h in range(KVH):
        for kv, ref in enumerate((pkeys_ref, pvalues_ref)):
            loads.append(pltpu.make_async_copy(
                ref.at[:, pl.ds(h * HD, HD)], bufs[kv].at[h, block(x, y)], load_sem.at[h * 2 + kv]))
    loads.append(pltpu.make_async_copy(query_ref, query, load_sem.at[8]))
    loads.append(pltpu.make_async_copy(keyval_ref, keyval, load_sem.at[9]))
    for c in loads:
        c.start()

    move = move_ref[0, 0]
    count = count_ref[0, 0]
    moved = (move < 3).astype(jnp.int32)
    kept = count - moved
    source = [jnp.minimum(move, 2)] + [j + (j >= move).astype(jnp.int32) for j in (0, 1)]

    def remote(h, kv, xx, yy, send_sem, recv_sem, to):
        ref = bufs[kv].at[h, block(xx, yy)]
        return pltpu.make_async_remote_copy(
            src_ref=ref, dst_ref=ref, send_sem=send_sem, recv_sem=recv_sem,
            device_id=to, device_id_type=MESH)

    def y_copy(h, kv, d):
        return remote(h, kv, x, y, y_send.at[h, kv, d - 1], y_recv.at[h, kv, y], above[d - 1])

    def x_copy(h, kv, yy, side):
        return remote(h, kv, x, yy, x_send.at[h, kv, yy, side], x_recv.at[h, kv, yy, side],
                      (right, left)[side])

    def relay_copy(h, kv, yy):
        xx = lax.rem(x + (3, 1)[kv], SIDE)
        return remote(h, kv, xx, yy, relay_send.at[h, kv, yy], relay_recv.at[h, kv, yy], (right, left)[kv])

    def wait_y(h, kv, d):
        yy = lax.rem(y + d, SIDE)
        remote(h, kv, x, yy, y_send.at[h, kv, 0], y_recv.at[h, kv, yy], right).wait_recv()
        return yy

    def wait_x(h, kv, yy, side):
        xx = lax.rem(x + (3, 1)[side], SIDE)
        remote(h, kv, xx, yy, x_send.at[h, kv, yy, side], x_recv.at[h, kv, yy, side], right).wait_recv()

    def wait_relay(h, kv, yy):
        xx = lax.rem(x + 2, SIDE)
        remote(h, kv, xx, yy, relay_send.at[h, kv, yy], relay_recv.at[h, kv, yy], right).wait_recv()

    def queries(h, i):
        c = h * 2 * HD
        return jnp.concatenate(
            [query[source[i], :, c:c + HD], query[source[i], :, c + HD:c + 2 * HD]], axis=0)

    def exponent(s):
        return jnp.exp(SOFTCAP * jnp.tanh(s * (HD ** -0.5 / SOFTCAP)))

    def first(h):
        c = h * HD
        row = lax.broadcasted_iota(jnp.int32, (2 * tokens, tokens), 0)
        key = lax.broadcasted_iota(jnp.int32, (2 * tokens, tokens), 1)
        allowed = key <= lax.rem(row, tokens)
        for i in range(3):
            kc = keyval[source[i], 0, :, c:c + HD]
            vc = keyval[source[i], 1, :, c:c + HD]
            s = lax.dot_general(queries(h, i), kc, NT, preferred_element_type=jnp.float32)
            e = jnp.where(allowed, exponent(s), 0.0)
            den[i] = e
            num[i] = jnp.dot(e.astype(jnp.bfloat16), vc, preferred_element_type=jnp.float32)

    def chunk(h, xx):
        part = pl.ds(pl.multiple_of(xx * col, col), col)
        for i in range(3):
            s = lax.dot_general(queries(h, i), kbuf[h, part], NT, preferred_element_type=jnp.float32)
            e = exponent(s)
            den[i] += e[:, :tokens] + e[:, tokens:]
            num[i] += jnp.dot(e.astype(jnp.bfloat16), vbuf[h, part], preferred_element_type=jnp.float32)

    def finish(h):
        for i in range(3):
            total = jnp.sum(den[i], axis=-1, keepdims=True)
            att = (num[i] / total).astype(jnp.bfloat16)
            for r in range(2):
                head = att[r * tokens:(r + 1) * tokens]
                c = (2 * h + r) * HD
                term = head[tokens - 1:].astype(jnp.float32) * weight_ref[:, c:c + HD].astype(jnp.float32)
                if h == 0 and r == 0:
                    sums[i] = term
                else:
                    sums[i] += term
                if i == 0:
                    sent[h, :, r * HD:(r + 1) * HD] = head * moved.astype(jnp.bfloat16)
                else:
                    own[i - 1, :, c:c + HD] = head
            if i == 0:
                guest_copy(h).start()

    def guest_copy(h):
        return pltpu.make_async_remote_copy(
            src_ref=sent.at[h], dst_ref=guest.at[h], send_sem=g_send.at[h], recv_sem=g_recv.at[h],
            device_id=ahead, device_id_type=MESH)

    pl.semaphore_wait(barrier, 7)

    def begin(h):
        for kv in range(2):
            loads[h * 2 + kv].wait()
            for d in (1, 3, 2):
                y_copy(h, kv, d).start()
            for side in range(2):
                x_copy(h, kv, y, side).start()

    def spread(h):
        for d in (1, 3, 2):
            for kv in range(2):
                yy = wait_y(h, kv, d)
                for side in range(2):
                    x_copy(h, kv, yy, side).start()

    def order(d):
        return lax.rem(y + d, SIDE)

    def pass_on(h, d):
        yy = order(d)
        wait_x(h, 0, yy, 0)
        relay_copy(h, 0, yy).start()
        wait_x(h, 1, yy, 1)
        relay_copy(h, 1, yy).start()

    for h in range(KVH):
        begin(h)
    loads[8].wait()
    loads[9].wait()
    spread(0)
    for h in range(KVH):
        first(h)
        if h + 1 < KVH:
            spread(h + 1)
        chunk(h, x)
        for d in (0, 1, 3, 2):
            pass_on(h, d)
        for d in (0, 1, 3, 2):
            wait_x(h, 1, order(d), 0)
        chunk(h, lax.rem(x + 3, SIDE))
        for d in (0, 1, 3, 2):
            wait_x(h, 0, order(d), 1)
        chunk(h, lax.rem(x + 1, SIDE))
        for d in (0, 1, 3, 2):
            for kv in range(2):
                wait_relay(h, kv, order(d))
        chunk(h, lax.rem(x + 2, SIDE))
        finish(h)

    slot = lax.broadcasted_iota(jnp.int32, (1, 3), 1)
    totals = [jnp.sum(sums[i], axis=-1, keepdims=True) for i in range(3)]
    place = slot - (slot > move).astype(jnp.int32)
    kept_score = jnp.where(place <= 0, totals[1], totals[2])
    score_ref[...] = jnp.where(
        slot == move, totals[0], jnp.where(slot < count, kept_score, 0.0))

    for h in range(KVH):
        guest_copy(h).wait_recv()
        for j in range(2):
            is_own = (kept > j).astype(jnp.bfloat16)
            is_guest = (kept == j).astype(jnp.bfloat16)
            c = h * 2 * HD
            att_ref[j, :, c:c + 2 * HD] = own[j, :, c:c + 2 * HD] * is_own + guest[h] * is_guest

    for h in range(KVH):
        guest_copy(h).wait_send()
        for kv in range(2):
            for d in (1, 2, 3):
                y_copy(h, kv, d).wait_send()
            for yy in range(SIDE):
                for side in range(2):
                    x_copy(h, kv, yy, side).wait_send()
                relay_copy(h, kv, yy).wait_send()


def body(
    passage_query, passage_keyval, prefix_keys, prefix_values, home_count, move_slot, score_weight
):
    query = passage_query[0, 0]
    keyval = passage_keyval[0, 0]
    slots, tokens, width = query.shape
    rows = prefix_keys.shape[1]
    lanes = lax.axis_size("lane")
    any_ = pl.BlockSpec(memory_space=pl.ANY)
    smem = pl.BlockSpec(memory_space=pltpu.SMEM)
    vmem = pl.BlockSpec(memory_space=pltpu.VMEM)
    bf16, f32 = jnp.bfloat16, jnp.float32
    dma = pltpu.SemaphoreType.DMA
    attended, scores = pl.pallas_call(
        kernel,
        out_shape=(
            jax.ShapeDtypeStruct((2, tokens, width), bf16),
            jax.ShapeDtypeStruct((1, slots), f32),
        ),
        in_specs=[any_, any_, any_, any_, smem, smem, vmem],
        out_specs=(vmem, vmem),
        scratch_shapes=[
            pltpu.VMEM((KVH, rows * lanes, HD), bf16),
            pltpu.VMEM((KVH, rows * lanes, HD), bf16),
            pltpu.VMEM(query.shape, bf16),
            pltpu.VMEM(keyval.shape, bf16),
            pltpu.VMEM((3, 2 * tokens, HD), f32),
            pltpu.VMEM((3, 2 * tokens, tokens), f32),
            pltpu.VMEM((2, tokens, width), bf16),
            pltpu.VMEM((KVH, tokens, 2 * HD), bf16),
            pltpu.VMEM((KVH, tokens, 2 * HD), bf16),
            pltpu.VMEM((3, 1, HD), f32),
            dma((10,)),
            dma((KVH, 2, 3)),
            dma((KVH, 2, SIDE, 2)),
            dma((KVH, 2, SIDE)),
            dma((KVH, 2, SIDE)),
            dma((KVH, 2, SIDE, 2)),
            dma((KVH, 2, SIDE)),
            dma((KVH,)),
            dma((KVH,)),
        ],
        compiler_params=pltpu.CompilerParams(
            collective_id=0, has_side_effects=True, vmem_limit_bytes=48 * 2**20),
    )(query, keyval, prefix_keys[0], prefix_values[0], home_count, move_slot, score_weight[None])
    return attended[None, None], scores[None]


def solution(mesh):
    in_specs = (
        P("grp", "lane", None, None, None),
        P("grp", "lane", None, None, None, None),
        P("grp", "lane", None),
        P("grp", "lane", None),
        P("grp", "lane"),
        P("grp", "lane"),
        P(),
    )
    out_specs = (P("grp", "lane", None, None, None), P("grp", "lane", None))
    return jax.shard_map(body, mesh=mesh, in_specs=in_specs, out_specs=out_specs, check_vma=False)
```

```python
import functools

import jax
import jax.numpy as jnp
from jax import lax
from jax.experimental import pallas as pl
from jax.experimental.pallas import tpu as pltpu
from jax.sharding import PartitionSpec as P

MESH = pl.DeviceIdType.MESH
HD = 256
KVH = 4
SIDE = 4
SOFTCAP = 50.0
GY = 2
GX = 5
NT = (((1,), (1,)), ((), ()))


def kernel(
    query_ref, keyval_ref, pkeys_ref, pvalues_ref, count_ref, move_ref, weight_ref,
    att_ref, score_ref,
    kbuf, vbuf, query, keyval, num, den, own, sent, guest, transit, sums,
    load_sem, y_send, x_send, relay_send, y_recv, x_recv, relay_recv, g_send, g_recv, t_send, t_recv, ready, hello, go, go_y,
):
    groups = lax.axis_size("grp")
    g = lax.axis_index("grp")
    lane = lax.axis_index("lane")
    x, y = lane // SIDE, lax.rem(lane, SIDE)
    tokens = query.shape[1]
    rows = pkeys_ref.shape[0]
    col = rows * SIDE
    bufs = (kbuf, vbuf)

    right = (g, lax.rem(x + 1, SIDE) * SIDE + y)
    left = (g, lax.rem(x + 3, SIDE) * SIDE + y)
    across = [(g, x * SIDE + lax.rem(y + d, SIDE)) for d in (1, 2, 3)]
    ahead = (lax.rem(g + 1, groups), lane)
    behind = (lax.rem(g + groups - 1, groups), lane)
    run = min(groups, 16)
    odd = lax.rem(g, 2)
    not_first = (lax.rem(g, run) > 0).astype(jnp.int32)
    not_last = (lax.rem(g, run) < run - 1).astype(jnp.int32)
    via = run > 2
    is_via = lax.rem(g, run) == 1
    closer = (g // run * run + run - 1, lane)
    stop = (g // run * run + 1, lane)
    landing = (lax.rem(g + run - 1, groups), lane)
    near = (y + 1 - 2 * lax.rem(y, 2), 2 - y // 2, 3 - 3 * (y // 2))

    barrier = pltpu.get_barrier_semaphore()

    def greet(other):
        pl.semaphore_signal(barrier, inc=1, device_id=other, device_id_type=MESH)

    for other in (right, left, *across):
        greet(other)
    pl.when(odd == 1)(lambda: greet(behind))
    pl.when((odd == 1) & (not_last == 1))(lambda: greet(ahead))
    pl.when((odd == 0) & (not_first == 0))(lambda: greet(behind))
    if via:
        pl.when(is_via)(lambda: greet(closer))

    def block(xx, yy):
        return pl.ds(pl.multiple_of((xx * SIDE + yy) * rows, rows), rows)

    loads = []
    for h in range(KVH):
        for kv, ref in enumerate((pkeys_ref, pvalues_ref)):
            loads.append(pltpu.make_async_copy(
                ref.at[:, pl.ds(h * HD, HD)], bufs[kv].at[h, block(x, y)], load_sem.at[h * 2 + kv]))
    loads.append(pltpu.make_async_copy(query_ref, query, load_sem.at[8]))
    loads.append(pltpu.make_async_copy(keyval_ref, keyval, load_sem.at[9]))
    for c in loads:
        c.start()

    move = move_ref[0, 0]
    count = count_ref[0, 0]
    moved = (move < 3).astype(jnp.int32)
    kept = count - moved
    source = [jnp.minimum(move, 2)] + [j + (j >= move).astype(jnp.int32) for j in (0, 1)]

    def remote(h, kv, xx, yy, send_sem, recv_sem, to):
        ref = bufs[kv].at[h, block(xx, yy)]
        return pltpu.make_async_remote_copy(
            src_ref=ref, dst_ref=ref, send_sem=send_sem, recv_sem=recv_sem,
            device_id=to, device_id_type=MESH)

    def y_copy(h, kv, d):
        return remote(h, kv, x, y, y_send.at[h, kv, d], y_recv.at[h, kv, y], across[d])

    def x_copy(h, kv, yy, side):
        return remote(h, kv, x, yy, x_send.at[h, kv, yy, side], x_recv.at[h, kv, yy, side],
                      (right, left)[side])

    def relay_copy(h, kv, yy):
        xx = lax.rem(x + (3, 1)[kv], SIDE)
        return remote(h, kv, xx, yy, relay_send.at[h, kv, yy], relay_recv.at[h, kv, yy], (right, left)[kv])

    def wait_y(h, kv, yy):
        remote(h, kv, x, yy, y_send.at[h, kv, 0], y_recv.at[h, kv, yy], right).wait_recv()

    def wait_x(h, kv, yy, side):
        xx = lax.rem(x + (3, 1)[side], SIDE)
        remote(h, kv, xx, yy, x_send.at[h, kv, yy, side], x_recv.at[h, kv, yy, side], right).wait_recv()

    def wait_relay(h, kv, yy):
        xx = lax.rem(x + 2, SIDE)
        remote(h, kv, xx, yy, relay_send.at[h, kv, yy], relay_recv.at[h, kv, yy], right).wait_recv()

    def queries(h, i):
        c = h * 2 * HD
        return jnp.concatenate(
            [query[source[i], :, c:c + HD], query[source[i], :, c + HD:c + 2 * HD]], axis=0)

    def exponent(s):
        return jnp.exp(SOFTCAP * jnp.tanh(s * (HD ** -0.5 / SOFTCAP)))

    def first(h):
        c = h * HD
        row = lax.broadcasted_iota(jnp.int32, (2 * tokens, tokens), 0)
        key = lax.broadcasted_iota(jnp.int32, (2 * tokens, tokens), 1)
        allowed = key <= lax.rem(row, tokens)
        for i in range(3):
            kc = keyval[source[i], 0, :, c:c + HD]
            vc = keyval[source[i], 1, :, c:c + HD]
            s = lax.dot_general(queries(h, i), kc, NT, preferred_element_type=jnp.float32)
            e = jnp.where(allowed, exponent(s), 0.0)
            den[i] = e
            num[i] = jnp.dot(e.astype(jnp.bfloat16), vc, preferred_element_type=jnp.float32)

    def chunk(h, xx):
        part = pl.ds(pl.multiple_of(xx * col, col), col)
        for i in range(3):
            s = lax.dot_general(queries(h, i), kbuf[h, part], NT, preferred_element_type=jnp.float32)
            e = exponent(s)
            den[i] += e[:, :tokens] + e[:, tokens:]
            num[i] += jnp.dot(e.astype(jnp.bfloat16), vbuf[h, part], preferred_element_type=jnp.float32)

    def finish(h):
        for i in range(3):
            total = jnp.sum(den[i], axis=-1, keepdims=True)
            att = (num[i] / total).astype(jnp.bfloat16)
            for r in range(2):
                head = att[r * tokens:(r + 1) * tokens]
                c = (2 * h + r) * HD
                term = head[tokens - 1:].astype(jnp.float32) * weight_ref[pl.ds(c, HD)].astype(jnp.float32).reshape(1, HD)
                if h == 0 and r == 0:
                    sums[i] = term
                else:
                    sums[i] += term
                if i == 0:
                    sent[h, :, r * HD:(r + 1) * HD] = head * moved.astype(jnp.bfloat16)
                else:
                    own[i - 1, :, c:c + HD] = head
            if i == 0:
                if via and h < KVH - 1:
                    pl.when(not_last == 1)(lambda: guest_copy(h).start())
                    pl.when(not_last == 0)(lambda: transit_copy(h).start())
                else:
                    guest_copy(h).start()

    def transit_copy(h):
        return pltpu.make_async_remote_copy(
            src_ref=sent.at[h], dst_ref=transit.at[h], send_sem=g_send.at[h], recv_sem=t_recv.at[h],
            device_id=stop, device_id_type=MESH)

    def landing_copy(h):
        return pltpu.make_async_remote_copy(
            src_ref=transit.at[h], dst_ref=guest.at[h], send_sem=t_send.at[h], recv_sem=g_recv.at[h],
            device_id=landing, device_id_type=MESH)

    def guest_copy(h):
        return pltpu.make_async_remote_copy(
            src_ref=sent.at[h], dst_ref=guest.at[h], send_sem=g_send.at[h], recv_sem=g_recv.at[h],
            device_id=ahead, device_id_type=MESH)

    pl.semaphore_wait(barrier, 5 + (1 - odd) * (1 + not_first) + odd * (1 - not_last) * (2 if via else 1))

    def tell(sem, other):
        pl.semaphore_signal(sem, inc=1, device_id=other, device_id_type=MESH)

    @pl.when(odd == 0)
    def _():
        tell(hello, ahead)
        pl.when(not_first == 1)(lambda: tell(ready, behind))

    def release(sem):
        pl.when(odd == 1)(lambda: tell(sem, behind))

    def begin(h):
        for kv in range(2):
            loads[h * 2 + kv].wait()
            for d in range(3):
                y_copy(h, kv, d).start()

    def begin_x(h):
        for kv in range(2):
            for side in range(2):
                x_copy(h, kv, y, side).start()

    def spread(h):
        for yy in near:
            for kv in range(2):
                wait_y(h, kv, yy)
                for side in range(2):
                    x_copy(h, kv, yy, side).start()

    order = (y, *near)

    def pass_on(h, i):
        yy = order[i]
        wait_x(h, 0, yy, 0)
        relay_copy(h, 0, yy).start()
        wait_x(h, 1, yy, 1)
        relay_copy(h, 1, yy).start()

    def work(h, i):
        if i == 0:
            first(h)
            chunk(h, x)
        if i == 1:
            for yy in order:
                wait_x(h, 1, yy, 0)
            chunk(h, lax.rem(x + 3, SIDE))
        if i == 2:
            for yy in order:
                wait_x(h, 0, yy, 1)
            chunk(h, lax.rem(x + 1, SIDE))
        if i == 3:
            for yy in order:
                for kv in range(2):
                    wait_relay(h, kv, yy)
            chunk(h, lax.rem(x + 2, SIDE))
            if h == 0:
                pl.when((odd == 1) & (not_last == 1))(lambda: pl.semaphore_wait(ready, 1))
            finish(h)

    pl.when((odd == 0) & (GY >= 0))(lambda: pl.semaphore_wait(go_y, 1))
    for h in range(KVH):
        begin(h)
    pl.when(odd == 1)(lambda: pl.semaphore_wait(hello, 1))
    pl.when((odd == 0) & (GX >= 0))(lambda: pl.semaphore_wait(go, 1))
    for h in range(KVH):
        begin_x(h)
    for h in range(2):
        spread(h)
        if GY == h:
            release(go_y)
        if GX == h:
            release(go)
    loads[8].wait()
    loads[9].wait()
    for h in range(KVH):
        for i in range(SIDE):
            pass_on(h, i)
            if h > 0:
                work(h - 1, i)
        if GX == h + 4:
            release(go)
        if h + 2 < KVH:
            spread(h + 2)
            if GY == h + 2:
                release(go_y)
    for i in range(SIDE):
        work(KVH - 1, i)

    if via:
        @pl.when(is_via)
        def _():
            for h in range(KVH - 1):
                transit_copy(h).wait_recv()
                landing_copy(h).start()

    slot = lax.broadcasted_iota(jnp.int32, (1, 3), 1)
    totals = [jnp.sum(sums[i], axis=-1, keepdims=True) for i in range(3)]
    place = slot - (slot > move).astype(jnp.int32)
    kept_score = jnp.where(place <= 0, totals[1], totals[2])
    score_ref[...] = jnp.where(
        slot == move, totals[0], jnp.where(slot < count, kept_score, 0.0))

    for h in range(KVH):
        guest_copy(h).wait_recv()
        for j in range(2):
            is_own = (kept > j).astype(jnp.bfloat16)
            is_guest = (kept == j).astype(jnp.bfloat16)
            c = h * 2 * HD
            att_ref[j, :, c:c + 2 * HD] = own[j, :, c:c + 2 * HD] * is_own + guest[h] * is_guest

    if via:
        @pl.when(is_via)
        def _():
            for h in range(KVH - 1):
                landing_copy(h).wait_send()

    for h in range(KVH):
        guest_copy(h).wait_send()
        for kv in range(2):
            for d in range(3):
                y_copy(h, kv, d).wait_send()
            for yy in range(SIDE):
                for side in range(2):
                    x_copy(h, kv, yy, side).wait_send()
                relay_copy(h, kv, yy).wait_send()


def body(
    passage_query, passage_keyval, prefix_keys, prefix_values, home_count, move_slot, score_weight
):
    query = passage_query[0, 0]
    keyval = passage_keyval[0, 0]
    slots, tokens, width = query.shape
    rows = prefix_keys.shape[1]
    lanes = lax.axis_size("lane")
    any_ = pl.BlockSpec(memory_space=pl.ANY)
    vmem = pl.BlockSpec(memory_space=pltpu.VMEM)
    bf16, f32 = jnp.bfloat16, jnp.float32
    dma = pltpu.SemaphoreType.DMA
    attended, scores = pl.pallas_call(
        kernel,
        out_shape=(
            jax.ShapeDtypeStruct((2, tokens, width), bf16),
            jax.ShapeDtypeStruct((1, slots), f32),
        ),
        in_specs=[any_, any_, any_, any_, vmem, vmem, vmem],
        out_specs=(vmem, vmem),
        scratch_shapes=[
            pltpu.VMEM((KVH, rows * lanes, HD), bf16),
            pltpu.VMEM((KVH, rows * lanes, HD), bf16),
            pltpu.VMEM(query.shape, bf16),
            pltpu.VMEM(keyval.shape, bf16),
            pltpu.VMEM((3, 2 * tokens, HD), f32),
            pltpu.VMEM((3, 2 * tokens, tokens), f32),
            pltpu.VMEM((2, tokens, width), bf16),
            pltpu.VMEM((KVH, tokens, 2 * HD), bf16),
            pltpu.VMEM((KVH, tokens, 2 * HD), bf16),
            pltpu.VMEM((KVH - 1, tokens, 2 * HD), bf16),
            pltpu.VMEM((3, 1, HD), f32),
            dma((10,)),
            dma((KVH, 2, 3)),
            dma((KVH, 2, SIDE, 2)),
            dma((KVH, 2, SIDE)),
            dma((KVH, 2, SIDE)),
            dma((KVH, 2, SIDE, 2)),
            dma((KVH, 2, SIDE)),
            dma((KVH,)),
            dma((KVH,)),
            dma((KVH - 1,)),
            dma((KVH - 1,)),
            pltpu.SemaphoreType.REGULAR,
            pltpu.SemaphoreType.REGULAR,
            pltpu.SemaphoreType.REGULAR,
            pltpu.SemaphoreType.REGULAR,
        ],
        compiler_params=pltpu.CompilerParams(
            collective_id=0, has_side_effects=True, vmem_limit_bytes=60 * 2**20),
    )(query, keyval, prefix_keys[0], prefix_values[0], home_count, move_slot, score_weight)
    return attended[None, None], scores[None]


def solution(mesh):
    in_specs = (
        P("grp", "lane", None, None, None),
        P("grp", "lane", None, None, None, None),
        P("grp", "lane", None),
        P("grp", "lane", None),
        P("grp", "lane"),
        P("grp", "lane"),
        P(),
    )
    out_specs = (P("grp", "lane", None, None, None), P("grp", "lane", None))
    return jax.shard_map(body, mesh=mesh, in_specs=in_specs, out_specs=out_specs, check_vma=False)
```

```python
import functools

import jax
import jax.numpy as jnp
from jax import lax
from jax.experimental import pallas as pl
from jax.experimental.pallas import tpu as pltpu
from jax.sharding import PartitionSpec as P

MESH = pl.DeviceIdType.MESH
HD = 256
KVH = 4
SIDE = 4
SOFTCAP = 50.0
GY = 2
VIA = 2
GX = 6
NT = (((1,), (1,)), ((), ()))


def kernel(
    query_ref, keyval_ref, pkeys_ref, pvalues_ref, count_ref, move_ref, weight_ref,
    att_ref, score_ref,
    kbuf, vbuf, query, keyval, num, den, own, sent, guest, transit, sums,
    load_sem, y_send, x_send, relay_send, y_recv, x_recv, relay_recv, g_send, g_recv, t_send, t_recv, ready, hello, go, go_y,
):
    groups = lax.axis_size("grp")
    g = lax.axis_index("grp")
    lane = lax.axis_index("lane")
    x, y = lane // SIDE, lax.rem(lane, SIDE)
    tokens = query.shape[1]
    rows = pkeys_ref.shape[0]
    col = rows * SIDE
    bufs = (kbuf, vbuf)

    right = (g, lax.rem(x + 1, SIDE) * SIDE + y)
    left = (g, lax.rem(x + 3, SIDE) * SIDE + y)
    across = [(g, x * SIDE + lax.rem(y + d, SIDE)) for d in (1, 2, 3)]
    ahead = (lax.rem(g + 1, groups), lane)
    behind = (lax.rem(g + groups - 1, groups), lane)
    run = min(groups, 16)
    odd = lax.rem(g, 2)
    not_first = (lax.rem(g, run) > 0).astype(jnp.int32)
    not_last = (lax.rem(g, run) < run - 1).astype(jnp.int32)
    via = run > 2
    is_via = lax.rem(g, run) == 1
    closer = (g // run * run + run - 1, lane)
    stop = (g // run * run + 1, lane)
    landing = (lax.rem(g + run - 1, groups), lane)
    near = (y + 1 - 2 * lax.rem(y, 2), 2 - y // 2, 3 - 3 * (y // 2))

    barrier = pltpu.get_barrier_semaphore()

    def greet(other):
        pl.semaphore_signal(barrier, inc=1, device_id=other, device_id_type=MESH)

    for other in (right, left, *across):
        greet(other)
    pl.when(odd == 1)(lambda: greet(behind))
    pl.when((odd == 1) & (not_last == 1))(lambda: greet(ahead))
    pl.when((odd == 0) & (not_first == 0))(lambda: greet(behind))
    if via:
        pl.when(is_via)(lambda: greet(closer))

    def block(xx, yy):
        return pl.ds(pl.multiple_of((xx * SIDE + yy) * rows, rows), rows)

    loads = []
    for h in range(KVH):
        for kv, ref in enumerate((pkeys_ref, pvalues_ref)):
            loads.append(pltpu.make_async_copy(
                ref.at[:, pl.ds(h * HD, HD)], bufs[kv].at[h, block(x, y)], load_sem.at[h * 2 + kv]))
    loads.append(pltpu.make_async_copy(query_ref, query, load_sem.at[8]))
    loads.append(pltpu.make_async_copy(keyval_ref, keyval, load_sem.at[9]))
    for c in loads:
        c.start()

    move = move_ref[0, 0]
    count = count_ref[0, 0]
    moved = (move < 3).astype(jnp.int32)
    kept = count - moved
    source = [jnp.minimum(move, 2)] + [j + (j >= move).astype(jnp.int32) for j in (0, 1)]

    def remote(h, kv, xx, yy, send_sem, recv_sem, to):
        ref = bufs[kv].at[h, block(xx, yy)]
        return pltpu.make_async_remote_copy(
            src_ref=ref, dst_ref=ref, send_sem=send_sem, recv_sem=recv_sem,
            device_id=to, device_id_type=MESH)

    def y_copy(h, kv, d):
        return remote(h, kv, x, y, y_send.at[h, kv, d], y_recv.at[h, kv, y], across[d])

    def x_copy(h, kv, yy, side):
        return remote(h, kv, x, yy, x_send.at[h, kv, yy, side], x_recv.at[h, kv, yy, side],
                      (right, left)[side])

    def relay_copy(h, kv, yy):
        xx = lax.rem(x + (3, 1)[kv], SIDE)
        return remote(h, kv, xx, yy, relay_send.at[h, kv, yy], relay_recv.at[h, kv, yy], (right, left)[kv])

    def wait_y(h, kv, yy):
        remote(h, kv, x, yy, y_send.at[h, kv, 0], y_recv.at[h, kv, yy], right).wait_recv()

    def wait_x(h, kv, yy, side):
        xx = lax.rem(x + (3, 1)[side], SIDE)
        remote(h, kv, xx, yy, x_send.at[h, kv, yy, side], x_recv.at[h, kv, yy, side], right).wait_recv()

    def wait_relay(h, kv, yy):
        xx = lax.rem(x + 2, SIDE)
        remote(h, kv, xx, yy, relay_send.at[h, kv, yy], relay_recv.at[h, kv, yy], right).wait_recv()

    def queries(h, i):
        c = h * 2 * HD
        return jnp.concatenate(
            [query[source[i], :, c:c + HD], query[source[i], :, c + HD:c + 2 * HD]], axis=0)

    def exponent(s):
        return jnp.exp(SOFTCAP * jnp.tanh(s * (HD ** -0.5 / SOFTCAP)))

    def first(h):
        c = h * HD
        row = lax.broadcasted_iota(jnp.int32, (2 * tokens, tokens), 0)
        key = lax.broadcasted_iota(jnp.int32, (2 * tokens, tokens), 1)
        allowed = key <= lax.rem(row, tokens)
        for i in range(3):
            kc = keyval[source[i], 0, :, c:c + HD]
            vc = keyval[source[i], 1, :, c:c + HD]
            s = lax.dot_general(queries(h, i), kc, NT, preferred_element_type=jnp.float32)
            e = jnp.where(allowed, exponent(s), 0.0)
            den[i] = e
            num[i] = jnp.dot(e.astype(jnp.bfloat16), vc, preferred_element_type=jnp.float32)

    def chunk(h, xx, slots=(0, 1, 2)):
        part = pl.ds(pl.multiple_of(xx * col, col), col)
        for i in slots:
            s = lax.dot_general(queries(h, i), kbuf[h, part], NT, preferred_element_type=jnp.float32)
            e = exponent(s)
            den[i] += e[:, :tokens] + e[:, tokens:]
            num[i] += jnp.dot(e.astype(jnp.bfloat16), vbuf[h, part], preferred_element_type=jnp.float32)

    def finish(h, slots):
        for i in slots:
            total = jnp.sum(den[i], axis=-1, keepdims=True)
            att = (num[i] / total).astype(jnp.bfloat16)
            for r in range(2):
                head = att[r * tokens:(r + 1) * tokens]
                c = (2 * h + r) * HD
                term = head[tokens - 1:].astype(jnp.float32) * weight_ref[pl.ds(c, HD)].astype(jnp.float32).reshape(1, HD)
                if h == 0 and r == 0:
                    sums[i] = term
                else:
                    sums[i] += term
                if i == 0:
                    sent[h, :, r * HD:(r + 1) * HD] = head * moved.astype(jnp.bfloat16)
                else:
                    own[i - 1, :, c:c + HD] = head
            if i == 0:
                if via and h < VIA:
                    pl.when(not_last == 1)(lambda: guest_copy(h).start())
                    pl.when(not_last == 0)(lambda: transit_copy(h).start())
                else:
                    guest_copy(h).start()

    def transit_copy(h):
        return pltpu.make_async_remote_copy(
            src_ref=sent.at[h], dst_ref=transit.at[h], send_sem=g_send.at[h], recv_sem=t_recv.at[h],
            device_id=stop, device_id_type=MESH)

    def landing_copy(h):
        return pltpu.make_async_remote_copy(
            src_ref=transit.at[h], dst_ref=guest.at[h], send_sem=t_send.at[h], recv_sem=g_recv.at[h],
            device_id=landing, device_id_type=MESH)

    def guest_copy(h):
        return pltpu.make_async_remote_copy(
            src_ref=sent.at[h], dst_ref=guest.at[h], send_sem=g_send.at[h], recv_sem=g_recv.at[h],
            device_id=ahead, device_id_type=MESH)

    pl.semaphore_wait(barrier, 5 + (1 - odd) * (1 + not_first) + odd * (1 - not_last) * (2 if via else 1))

    def tell(sem, other):
        pl.semaphore_signal(sem, inc=1, device_id=other, device_id_type=MESH)

    @pl.when(odd == 0)
    def _():
        tell(hello, ahead)
        pl.when(not_first == 1)(lambda: tell(ready, behind))

    def release(sem):
        pl.when(odd == 1)(lambda: tell(sem, behind))

    def begin(h):
        for kv in range(2):
            loads[h * 2 + kv].wait()
            for d in range(3):
                y_copy(h, kv, d).start()

    def begin_x(h):
        for kv in range(2):
            for side in range(2):
                x_copy(h, kv, y, side).start()

    def spread(h):
        for yy in near:
            for kv in range(2):
                wait_y(h, kv, yy)
                for side in range(2):
                    x_copy(h, kv, yy, side).start()

    order = (y, *near)

    def pass_on(h, i):
        yy = order[i]
        wait_x(h, 0, yy, 0)
        relay_copy(h, 0, yy).start()
        wait_x(h, 1, yy, 1)
        relay_copy(h, 1, yy).start()

    def work(h, i):
        if i == 0:
            first(h)
            chunk(h, x)
        if i == 1:
            for yy in order:
                wait_x(h, 1, yy, 0)
            chunk(h, lax.rem(x + 3, SIDE))
        if i == 2:
            for yy in order:
                wait_x(h, 0, yy, 1)
            chunk(h, lax.rem(x + 1, SIDE))
        if i == 3:
            for yy in order:
                for kv in range(2):
                    wait_relay(h, kv, yy)
            if h == 0:
                pl.when((odd == 1) & (not_last == 1))(lambda: pl.semaphore_wait(ready, 1))
            for slots in ((0,), (1, 2)):
                chunk(h, lax.rem(x + 2, SIDE), slots)
                finish(h, slots)

    pl.when((odd == 0) & (GY >= 0))(lambda: pl.semaphore_wait(go_y, 1))
    for h in range(KVH):
        begin(h)
    pl.when((odd == 0) & (GX >= 0))(lambda: pl.semaphore_wait(go, 1))
    for h in range(KVH):
        begin_x(h)
    for h in range(2):
        spread(h)
        if GY == h:
            release(go_y)
        if GX == h:
            release(go)
    loads[8].wait()
    loads[9].wait()
    for h in range(KVH):
        for i in range(SIDE):
            pass_on(h, i)
            if h > 0:
                work(h - 1, i)
        if GX == h + 4:
            release(go)
        if h + 2 < KVH:
            spread(h + 2)
            if GY == h + 2:
                pl.when(odd == 1)(lambda: pl.semaphore_wait(hello, 1))
                release(go_y)
    for i in range(SIDE):
        work(KVH - 1, i)

    if via:
        @pl.when(is_via)
        def _():
            for h in range(VIA):
                transit_copy(h).wait_recv()
                landing_copy(h).start()

    slot = lax.broadcasted_iota(jnp.int32, (1, 3), 1)
    totals = [jnp.sum(sums[i], axis=-1, keepdims=True) for i in range(3)]
    place = slot - (slot > move).astype(jnp.int32)
    kept_score = jnp.where(place <= 0, totals[1], totals[2])
    score_ref[...] = jnp.where(
        slot == move, totals[0], jnp.where(slot < count, kept_score, 0.0))

    for h in range(KVH):
        guest_copy(h).wait_recv()
        for j in range(2):
            is_own = (kept > j).astype(jnp.bfloat16)
            is_guest = (kept == j).astype(jnp.bfloat16)
            c = h * 2 * HD
            att_ref[j, :, c:c + 2 * HD] = own[j, :, c:c + 2 * HD] * is_own + guest[h] * is_guest

    if via:
        @pl.when(is_via)
        def _():
            for h in range(VIA):
                landing_copy(h).wait_send()

    for h in range(KVH):
        guest_copy(h).wait_send()
        for kv in range(2):
            for d in range(3):
                y_copy(h, kv, d).wait_send()
            for yy in range(SIDE):
                for side in range(2):
                    x_copy(h, kv, yy, side).wait_send()
                relay_copy(h, kv, yy).wait_send()


def body(
    passage_query, passage_keyval, prefix_keys, prefix_values, home_count, move_slot, score_weight
):
    query = passage_query[0, 0]
    keyval = passage_keyval[0, 0]
    slots, tokens, width = query.shape
    rows = prefix_keys.shape[1]
    lanes = lax.axis_size("lane")
    any_ = pl.BlockSpec(memory_space=pl.ANY)
    vmem = pl.BlockSpec(memory_space=pltpu.VMEM)
    bf16, f32 = jnp.bfloat16, jnp.float32
    dma = pltpu.SemaphoreType.DMA
    attended, scores = pl.pallas_call(
        kernel,
        out_shape=(
            pltpu.VMEM((2, tokens, width), bf16),
            pltpu.VMEM((1, slots), f32),
        ),
        in_specs=[any_, any_, any_, any_, vmem, vmem, vmem],
        out_specs=(vmem, vmem),
        scratch_shapes=[
            pltpu.VMEM((KVH, rows * lanes, HD), bf16),
            pltpu.VMEM((KVH, rows * lanes, HD), bf16),
            pltpu.VMEM(query.shape, bf16),
            pltpu.VMEM(keyval.shape, bf16),
            pltpu.VMEM((3, 2 * tokens, HD), f32),
            pltpu.VMEM((3, 2 * tokens, tokens), f32),
            pltpu.VMEM((2, tokens, width), bf16),
            pltpu.VMEM((KVH, tokens, 2 * HD), bf16),
            pltpu.VMEM((KVH, tokens, 2 * HD), bf16),
            pltpu.VMEM((VIA, tokens, 2 * HD), bf16),
            pltpu.VMEM((3, 1, HD), f32),
            dma((10,)),
            dma((KVH, 2, 3)),
            dma((KVH, 2, SIDE, 2)),
            dma((KVH, 2, SIDE)),
            dma((KVH, 2, SIDE)),
            dma((KVH, 2, SIDE, 2)),
            dma((KVH, 2, SIDE)),
            dma((KVH,)),
            dma((KVH,)),
            dma((VIA,)),
            dma((VIA,)),
            pltpu.SemaphoreType.REGULAR,
            pltpu.SemaphoreType.REGULAR,
            pltpu.SemaphoreType.REGULAR,
            pltpu.SemaphoreType.REGULAR,
        ],
        compiler_params=pltpu.CompilerParams(
            collective_id=0, has_side_effects=True, vmem_limit_bytes=60 * 2**20),
    )(query, keyval, prefix_keys[0], prefix_values[0], home_count, move_slot, score_weight)
    return attended[None, None], scores[None]


def solution(mesh):
    in_specs = (
        P("grp", "lane", None, None, None),
        P("grp", "lane", None, None, None, None),
        P("grp", "lane", None),
        P("grp", "lane", None),
        P("grp", "lane"),
        P("grp", "lane"),
        P(),
    )
    out_specs = (P("grp", "lane", None, None, None), P("grp", "lane", None))
    return jax.shard_map(body, mesh=mesh, in_specs=in_specs, out_specs=out_specs, check_vma=False)
```

```python
import functools

import jax
import jax.numpy as jnp
from jax import lax
from jax.experimental import pallas as pl
from jax.experimental.pallas import tpu as pltpu
from jax.sharding import PartitionSpec as P

MESH = pl.DeviceIdType.MESH
HD = 256
KVH = 4
SIDE = 4
SOFTCAP = 50.0
GY = 2
VIA = 2
GX = 6
NT = (((1,), (1,)), ((), ()))


def kernel(
    query_ref, keyval_ref, pkeys_ref, pvalues_ref, count_ref, move_ref, weight_hbm,
    att_ref, score_ref,
    kbuf, vbuf, query, keyval, num, den, own, sent, guest, transit, sums, weight_ref,
    load_sem, y_send, x_send, relay_send, y_recv, x_recv, relay_recv, g_send, g_recv, t_send, t_recv, ready, hello, go, go_y,
):
    groups = lax.axis_size("grp")
    g = lax.axis_index("grp")
    lane = lax.axis_index("lane")
    x, y = lane // SIDE, lax.rem(lane, SIDE)
    tokens = query.shape[1]
    rows = pkeys_ref.shape[0]
    col = rows * SIDE
    bufs = (kbuf, vbuf)

    right = (g, lax.rem(x + 1, SIDE) * SIDE + y)
    left = (g, lax.rem(x + 3, SIDE) * SIDE + y)
    ahead = (lax.rem(g + 1, groups), lane)
    behind = (lax.rem(g + groups - 1, groups), lane)
    run = min(groups, 16)
    odd = lax.rem(g, 2)
    not_first = (lax.rem(g, run) > 0).astype(jnp.int32)
    not_last = (lax.rem(g, run) < run - 1).astype(jnp.int32)
    via = run > 2
    is_via = lax.rem(g, run) == 1
    closer = (g // run * run + run - 1, lane)
    stop = (g // run * run + 1, lane)
    landing = (lax.rem(g + run - 1, groups), lane)
    near = (y + 1 - 2 * lax.rem(y, 2), 2 - y // 2, 3 - 3 * (y // 2))
    across = [(g, x * SIDE + yy) for yy in near]

    barrier = pltpu.get_barrier_semaphore()

    def greet(other):
        pl.semaphore_signal(barrier, inc=1, device_id=other, device_id_type=MESH)

    for other in (right, left, *across):
        greet(other)
    pl.when(odd == 1)(lambda: greet(behind))
    pl.when((odd == 1) & (not_last == 1))(lambda: greet(ahead))
    pl.when((odd == 0) & (not_first == 0))(lambda: greet(behind))
    if via:
        pl.when(is_via)(lambda: greet(closer))

    def block(xx, yy):
        return pl.ds(pl.multiple_of((xx * SIDE + yy) * rows, rows), rows)

    loads = []
    for h in range(KVH):
        for kv, ref in enumerate((pkeys_ref, pvalues_ref)):
            loads.append(pltpu.make_async_copy(
                ref.at[:, pl.ds(h * HD, HD)], bufs[kv].at[h, block(x, y)], load_sem.at[h * 2 + kv]))
    loads.append(pltpu.make_async_copy(query_ref, query, load_sem.at[8]))
    loads.append(pltpu.make_async_copy(keyval_ref, keyval, load_sem.at[9]))
    loads.append(pltpu.make_async_copy(weight_hbm, weight_ref, load_sem.at[10]))
    for c in loads:
        c.start()

    move = move_ref[0, 0]
    count = count_ref[0, 0]
    moved = (move < 3).astype(jnp.int32)
    kept = count - moved
    source = [jnp.minimum(move, 2)] + [j + (j >= move).astype(jnp.int32) for j in (0, 1)]

    def remote(h, kv, xx, yy, send_sem, recv_sem, to):
        ref = bufs[kv].at[h, block(xx, yy)]
        return pltpu.make_async_remote_copy(
            src_ref=ref, dst_ref=ref, send_sem=send_sem, recv_sem=recv_sem,
            device_id=to, device_id_type=MESH)

    def y_copy(h, kv, d):
        return remote(h, kv, x, y, y_send.at[h, kv, d], y_recv.at[h, kv, y], across[d])

    def x_copy(h, kv, yy, side):
        return remote(h, kv, x, yy, x_send.at[h, kv, yy, side], x_recv.at[h, kv, yy, side],
                      (right, left)[side])

    def relay_copy(h, kv, yy):
        xx = lax.rem(x + (3, 1)[kv], SIDE)
        return remote(h, kv, xx, yy, relay_send.at[h, kv, yy], relay_recv.at[h, kv, yy], (right, left)[kv])

    def wait_y(h, kv, yy):
        remote(h, kv, x, yy, y_send.at[h, kv, 0], y_recv.at[h, kv, yy], right).wait_recv()

    def wait_x(h, kv, yy, side):
        xx = lax.rem(x + (3, 1)[side], SIDE)
        remote(h, kv, xx, yy, x_send.at[h, kv, yy, side], x_recv.at[h, kv, yy, side], right).wait_recv()

    def wait_relay(h, kv, yy):
        xx = lax.rem(x + 2, SIDE)
        remote(h, kv, xx, yy, relay_send.at[h, kv, yy], relay_recv.at[h, kv, yy], right).wait_recv()

    def queries(h, i):
        c = h * 2 * HD
        return jnp.concatenate(
            [query[source[i], :, c:c + HD], query[source[i], :, c + HD:c + 2 * HD]], axis=0)

    def exponent(s):
        return jnp.exp(SOFTCAP * jnp.tanh(s * (HD ** -0.5 / SOFTCAP)))

    def first(h):
        c = h * HD
        row = lax.broadcasted_iota(jnp.int32, (2 * tokens, tokens), 0)
        key = lax.broadcasted_iota(jnp.int32, (2 * tokens, tokens), 1)
        allowed = key <= lax.rem(row, tokens)
        for i in range(3):
            kc = keyval[source[i], 0, :, c:c + HD]
            vc = keyval[source[i], 1, :, c:c + HD]
            s = lax.dot_general(queries(h, i), kc, NT, preferred_element_type=jnp.float32)
            e = jnp.where(allowed, exponent(s), 0.0)
            den[i] = e
            num[i] = jnp.dot(e.astype(jnp.bfloat16), vc, preferred_element_type=jnp.float32)

    def chunk(h, xx, slots=(0, 1, 2)):
        part = pl.ds(pl.multiple_of(xx * col, col), col)
        for i in slots:
            s = lax.dot_general(queries(h, i), kbuf[h, part], NT, preferred_element_type=jnp.float32)
            e = exponent(s)
            den[i] += e[:, :tokens] + e[:, tokens:]
            num[i] += jnp.dot(e.astype(jnp.bfloat16), vbuf[h, part], preferred_element_type=jnp.float32)

    def finish(h, slots):
        for i in slots:
            total = jnp.sum(den[i], axis=-1, keepdims=True)
            att = (num[i] / total).astype(jnp.bfloat16)
            for r in range(2):
                head = att[r * tokens:(r + 1) * tokens]
                c = (2 * h + r) * HD
                term = head[tokens - 1:].astype(jnp.float32) * weight_ref[pl.ds(c, HD)].astype(jnp.float32).reshape(1, HD)
                if h == 0 and r == 0:
                    sums[i] = term
                else:
                    sums[i] += term
                if i == 0:
                    sent[h, :, r * HD:(r + 1) * HD] = head * moved.astype(jnp.bfloat16)
                else:
                    own[i - 1, :, c:c + HD] = head
            if i == 0:
                if via and h < VIA:
                    pl.when(not_last == 1)(lambda: guest_copy(h).start())
                    pl.when(not_last == 0)(lambda: transit_copy(h).start())
                else:
                    guest_copy(h).start()

    def transit_copy(h):
        return pltpu.make_async_remote_copy(
            src_ref=sent.at[h], dst_ref=transit.at[h], send_sem=g_send.at[h], recv_sem=t_recv.at[h],
            device_id=stop, device_id_type=MESH)

    def landing_copy(h):
        return pltpu.make_async_remote_copy(
            src_ref=transit.at[h], dst_ref=guest.at[h], send_sem=t_send.at[h], recv_sem=g_recv.at[h],
            device_id=landing, device_id_type=MESH)

    def guest_copy(h):
        return pltpu.make_async_remote_copy(
            src_ref=sent.at[h], dst_ref=guest.at[h], send_sem=g_send.at[h], recv_sem=g_recv.at[h],
            device_id=ahead, device_id_type=MESH)

    pl.semaphore_wait(barrier, 5 + (1 - odd) * (1 + not_first) + odd * (1 - not_last) * (2 if via else 1))

    def tell(sem, other):
        pl.semaphore_signal(sem, inc=1, device_id=other, device_id_type=MESH)

    @pl.when(odd == 0)
    def _():
        tell(hello, ahead)
        pl.when(not_first == 1)(lambda: tell(ready, behind))

    def release(sem):
        pl.when(odd == 1)(lambda: tell(sem, behind))

    def begin(h):
        for d in range(3):
            for kv in range(2):
                y_copy(h, kv, d).start()

    def begin_x(h):
        for kv in range(2):
            loads[h * 2 + kv].wait()
            for side in range(2):
                x_copy(h, kv, y, side).start()

    def spread(h):
        for yy in near:
            for kv in range(2):
                wait_y(h, kv, yy)
                for side in range(2):
                    x_copy(h, kv, yy, side).start()

    order = (y, *near)

    def pass_on(h, i):
        yy = order[i]
        wait_x(h, 0, yy, 0)
        relay_copy(h, 0, yy).start()
        wait_x(h, 1, yy, 1)
        relay_copy(h, 1, yy).start()

    def work(h, i):
        if i == 0:
            first(h)
            chunk(h, x)
        if i == 1:
            for yy in order:
                wait_x(h, 1, yy, 0)
            chunk(h, lax.rem(x + 3, SIDE))
        if i == 2:
            for yy in order:
                wait_x(h, 0, yy, 1)
            chunk(h, lax.rem(x + 1, SIDE))
        if i == 3:
            for yy in order:
                for kv in range(2):
                    wait_relay(h, kv, yy)
            if h == 0:
                pl.when((odd == 1) & (not_last == 1))(lambda: pl.semaphore_wait(ready, 1))
            for slots in ((0,), (1, 2)):
                chunk(h, lax.rem(x + 2, SIDE), slots)
                finish(h, slots)

    for h in range(KVH):
        begin_x(h)
        pl.when(odd == 1)(functools.partial(begin, h))
    @pl.when(odd == 0)
    def _():
        pl.semaphore_wait(go_y, 1)
        for h in range(KVH):
            begin(h)
        pl.semaphore_wait(go, 1)

    for h in range(2):
        spread(h)
        if GY == h:
            release(go_y)
        if GX == h:
            release(go)
    loads[8].wait()
    loads[9].wait()
    loads[10].wait()
    for h in range(KVH):
        for i in range(SIDE):
            pass_on(h, i)
            if h > 0:
                work(h - 1, i)
        if GX == h + 4:
            release(go)
        if h + 2 < KVH:
            spread(h + 2)
            if GY == h + 2:
                pl.when(odd == 1)(lambda: pl.semaphore_wait(hello, 1))
                release(go_y)
    for i in range(SIDE):
        work(KVH - 1, i)

    if via:
        @pl.when(is_via)
        def _():
            for h in range(VIA):
                transit_copy(h).wait_recv()
                landing_copy(h).start()

    slot = lax.broadcasted_iota(jnp.int32, (1, 3), 1)
    totals = [jnp.sum(sums[i], axis=-1, keepdims=True) for i in range(3)]
    place = slot - (slot > move).astype(jnp.int32)
    kept_score = jnp.where(place <= 0, totals[1], totals[2])
    score_ref[...] = jnp.where(
        slot == move, totals[0], jnp.where(slot < count, kept_score, 0.0))

    for h in range(KVH):
        guest_copy(h).wait_recv()
        for j in range(2):
            is_own = (kept > j).astype(jnp.bfloat16)
            is_guest = (kept == j).astype(jnp.bfloat16)
            c = h * 2 * HD
            att_ref[j, :, c:c + 2 * HD] = own[j, :, c:c + 2 * HD] * is_own + guest[h] * is_guest

    if via:
        @pl.when(is_via)
        def _():
            for h in range(VIA):
                landing_copy(h).wait_send()

    for h in range(KVH):
        guest_copy(h).wait_send()
        for kv in range(2):
            for d in range(3):
                y_copy(h, kv, d).wait_send()
            for yy in range(SIDE):
                for side in range(2):
                    x_copy(h, kv, yy, side).wait_send()
                relay_copy(h, kv, yy).wait_send()


def body(
    passage_query, passage_keyval, prefix_keys, prefix_values, home_count, move_slot, score_weight
):
    query = passage_query[0, 0]
    keyval = passage_keyval[0, 0]
    slots, tokens, width = query.shape
    rows = prefix_keys.shape[1]
    lanes = lax.axis_size("lane")
    any_ = pl.BlockSpec(memory_space=pl.ANY)
    smem = pl.BlockSpec(memory_space=pltpu.SMEM)
    vmem = pl.BlockSpec(memory_space=pltpu.VMEM)
    bf16, f32 = jnp.bfloat16, jnp.float32
    dma = pltpu.SemaphoreType.DMA
    attended, scores = pl.pallas_call(
        kernel,
        out_shape=(
            pltpu.VMEM((2, tokens, width), bf16),
            pltpu.VMEM((1, slots), f32),
        ),
        in_specs=[any_, any_, any_, any_, smem, smem, any_],
        out_specs=(vmem, vmem),
        scratch_shapes=[
            pltpu.VMEM((KVH, rows * lanes, HD), bf16),
            pltpu.VMEM((KVH, rows * lanes, HD), bf16),
            pltpu.VMEM(query.shape, bf16),
            pltpu.VMEM(keyval.shape, bf16),
            pltpu.VMEM((3, 2 * tokens, HD), f32),
            pltpu.VMEM((3, 2 * tokens, tokens), f32),
            pltpu.VMEM((2, tokens, width), bf16),
            pltpu.VMEM((KVH, tokens, 2 * HD), bf16),
            pltpu.VMEM((KVH, tokens, 2 * HD), bf16),
            pltpu.VMEM((VIA, tokens, 2 * HD), bf16),
            pltpu.VMEM((3, 1, HD), f32),
            pltpu.VMEM(score_weight.shape, bf16),
            dma((11,)),
            dma((KVH, 2, 3)),
            dma((KVH, 2, SIDE, 2)),
            dma((KVH, 2, SIDE)),
            dma((KVH, 2, SIDE)),
            dma((KVH, 2, SIDE, 2)),
            dma((KVH, 2, SIDE)),
            dma((KVH,)),
            dma((KVH,)),
            dma((VIA,)),
            dma((VIA,)),
            pltpu.SemaphoreType.REGULAR,
            pltpu.SemaphoreType.REGULAR,
            pltpu.SemaphoreType.REGULAR,
            pltpu.SemaphoreType.REGULAR,
        ],
        compiler_params=pltpu.CompilerParams(
            collective_id=0, has_side_effects=True, vmem_limit_bytes=60 * 2**20),
    )(query, keyval, prefix_keys[0], prefix_values[0], home_count, move_slot, score_weight)
    return attended[None, None], scores[None]


def solution(mesh):
    in_specs = (
        P("grp", "lane", None, None, None),
        P("grp", "lane", None, None, None, None),
        P("grp", "lane", None),
        P("grp", "lane", None),
        P("grp", "lane"),
        P("grp", "lane"),
        P(),
    )
    out_specs = (P("grp", "lane", None, None, None), P("grp", "lane", None))
    return jax.shard_map(body, mesh=mesh, in_specs=in_specs, out_specs=out_specs, check_vma=False)
```

```python
import functools

import jax
import jax.numpy as jnp
from jax import lax
from jax.experimental import pallas as pl
from jax.experimental.pallas import tpu as pltpu
from jax.sharding import PartitionSpec as P

MESH = pl.DeviceIdType.MESH
HD = 256
KVH = 4
SIDE = 4
SOFTCAP = 50.0
GY = 2
VIA = 2
GX = 6
NT = (((1,), (1,)), ((), ()))


def kernel(
    query_ref, keyval_ref, pkeys_ref, pvalues_ref, count_ref, move_ref, weight_hbm,
    att_ref, score_ref,
    kbuf, vbuf, query, keyval, num, den, own, sent, guest, transit, sums, weight_ref,
    load_sem, y_send, x_send, relay_send, y_recv, x_recv, relay_recv, g_send, g_recv, t_send, t_recv, ready, hello, go, go_y,
):
    groups = lax.axis_size("grp")
    g = lax.axis_index("grp")
    lane = lax.axis_index("lane")
    x, y = lane // SIDE, lax.rem(lane, SIDE)
    tokens = query.shape[1]
    rows = pkeys_ref.shape[0]
    col = rows * SIDE
    bufs = (kbuf, vbuf)

    right = (g, lax.rem(x + 1, SIDE) * SIDE + y)
    left = (g, lax.rem(x + 3, SIDE) * SIDE + y)
    ahead = (lax.rem(g + 1, groups), lane)
    behind = (lax.rem(g + groups - 1, groups), lane)
    run = min(groups, 16)
    odd = lax.rem(g, 2)
    not_first = (lax.rem(g, run) > 0).astype(jnp.int32)
    not_last = (lax.rem(g, run) < run - 1).astype(jnp.int32)
    via = run > 2
    is_via = lax.rem(g, run) == 1
    closer = (g // run * run + run - 1, lane)
    stop = (g // run * run + 1, lane)
    landing = (lax.rem(g + run - 1, groups), lane)
    near = (y + 1 - 2 * lax.rem(y, 2), 2 - y // 2, 3 - 3 * (y // 2))
    across = [(g, x * SIDE + yy) for yy in near]

    barrier = pltpu.get_barrier_semaphore()

    def greet(other):
        pl.semaphore_signal(barrier, inc=1, device_id=other, device_id_type=MESH)

    for other in (right, left, *across):
        greet(other)
    pl.when(odd == 1)(lambda: greet(behind))
    pl.when((odd == 1) & (not_last == 1))(lambda: greet(ahead))
    pl.when((odd == 0) & (not_first == 0))(lambda: greet(behind))
    if via:
        pl.when(is_via)(lambda: greet(closer))

    def block(xx, yy):
        return pl.ds(pl.multiple_of((xx * SIDE + yy) * rows, rows), rows)

    loads = []
    for h in range(KVH):
        for kv, ref in enumerate((pkeys_ref, pvalues_ref)):
            loads.append(pltpu.make_async_copy(
                ref.at[:, pl.ds(h * HD, HD)], bufs[kv].at[h, block(x, y)], load_sem.at[h * 2 + kv]))
    loads.append(pltpu.make_async_copy(query_ref, query, load_sem.at[8]))
    loads.append(pltpu.make_async_copy(keyval_ref, keyval, load_sem.at[9]))
    loads.append(pltpu.make_async_copy(weight_hbm, weight_ref, load_sem.at[10]))
    for c in loads:
        c.start()

    move = move_ref[0, 0]
    count = count_ref[0, 0]
    moved = (move < 3).astype(jnp.int32)
    kept = count - moved
    source = [jnp.minimum(move, 2)] + [j + (j >= move).astype(jnp.int32) for j in (0, 1)]

    def remote(h, kv, xx, yy, send_sem, recv_sem, to):
        ref = bufs[kv].at[h, block(xx, yy)]
        return pltpu.make_async_remote_copy(
            src_ref=ref, dst_ref=ref, send_sem=send_sem, recv_sem=recv_sem,
            device_id=to, device_id_type=MESH)

    def y_copy(h, kv, d):
        return remote(h, kv, x, y, y_send.at[h, kv, d], y_recv.at[h, kv, y], across[d])

    def x_copy(h, kv, yy, side):
        return remote(h, kv, x, yy, x_send.at[h, kv, yy, side], x_recv.at[h, kv, yy, side],
                      (right, left)[side])

    def relay_copy(h, kv, yy):
        xx = lax.rem(x + (3, 1)[kv], SIDE)
        return remote(h, kv, xx, yy, relay_send.at[h, kv, yy], relay_recv.at[h, kv, yy], (right, left)[kv])

    def wait_y(h, kv, yy):
        remote(h, kv, x, yy, y_send.at[h, kv, 0], y_recv.at[h, kv, yy], right).wait_recv()

    def wait_x(h, kv, yy, side):
        xx = lax.rem(x + (3, 1)[side], SIDE)
        remote(h, kv, xx, yy, x_send.at[h, kv, yy, side], x_recv.at[h, kv, yy, side], right).wait_recv()

    def wait_relay(h, kv, yy):
        xx = lax.rem(x + 2, SIDE)
        remote(h, kv, xx, yy, relay_send.at[h, kv, yy], relay_recv.at[h, kv, yy], right).wait_recv()

    def queries(h, i):
        c = h * 2 * HD
        return jnp.concatenate(
            [query[source[i], :, c:c + HD], query[source[i], :, c + HD:c + 2 * HD]], axis=0)

    def exponent(s):
        return jnp.exp(SOFTCAP * jnp.tanh(s * (HD ** -0.5 / SOFTCAP)))

    def first(h):
        c = h * HD
        row = lax.broadcasted_iota(jnp.int32, (2 * tokens, tokens), 0)
        key = lax.broadcasted_iota(jnp.int32, (2 * tokens, tokens), 1)
        allowed = key <= lax.rem(row, tokens)
        for i in range(3):
            kc = keyval[source[i], 0, :, c:c + HD]
            vc = keyval[source[i], 1, :, c:c + HD]
            s = lax.dot_general(queries(h, i), kc, NT, preferred_element_type=jnp.float32)
            e = jnp.where(allowed, exponent(s), 0.0)
            den[i] = e
            num[i] = jnp.dot(e.astype(jnp.bfloat16), vc, preferred_element_type=jnp.float32)

    def chunk(h, xx, slots=(0, 1, 2)):
        part = pl.ds(pl.multiple_of(xx * col, col), col)
        for i in slots:
            s = lax.dot_general(queries(h, i), kbuf[h, part], NT, preferred_element_type=jnp.float32)
            e = exponent(s)
            den[i] += e[:, :tokens] + e[:, tokens:]
            num[i] += jnp.dot(e.astype(jnp.bfloat16), vbuf[h, part], preferred_element_type=jnp.float32)

    def finish(h, slots):
        for i in slots:
            total = jnp.sum(den[i], axis=-1, keepdims=True)
            att = (num[i] / total).astype(jnp.bfloat16)
            for r in range(2):
                head = att[r * tokens:(r + 1) * tokens]
                c = (2 * h + r) * HD
                term = head[tokens - 1:].astype(jnp.float32) * weight_ref[pl.ds(c, HD)].astype(jnp.float32).reshape(1, HD)
                if h == 0 and r == 0:
                    sums[i] = term
                else:
                    sums[i] += term
                if i == 0:
                    sent[h, :, r * HD:(r + 1) * HD] = head * moved.astype(jnp.bfloat16)
                else:
                    own[i - 1, :, c:c + HD] = head
            if i == 0:
                if via and h < VIA:
                    pl.when(not_last == 1)(lambda: guest_copy(h).start())
                    pl.when(not_last == 0)(lambda: transit_copy(h).start())
                else:
                    guest_copy(h).start()

    def transit_copy(h):
        return pltpu.make_async_remote_copy(
            src_ref=sent.at[h], dst_ref=transit.at[h], send_sem=g_send.at[h], recv_sem=t_recv.at[h],
            device_id=stop, device_id_type=MESH)

    def landing_copy(h):
        return pltpu.make_async_remote_copy(
            src_ref=transit.at[h], dst_ref=guest.at[h], send_sem=t_send.at[h], recv_sem=g_recv.at[h],
            device_id=landing, device_id_type=MESH)

    def guest_copy(h):
        return pltpu.make_async_remote_copy(
            src_ref=sent.at[h], dst_ref=guest.at[h], send_sem=g_send.at[h], recv_sem=g_recv.at[h],
            device_id=ahead, device_id_type=MESH)

    pl.semaphore_wait(barrier, 5 + (1 - odd) * (1 + not_first) + odd * (1 - not_last) * (2 if via else 1))

    def tell(sem, other):
        pl.semaphore_signal(sem, inc=1, device_id=other, device_id_type=MESH)

    @pl.when(odd == 0)
    def _():
        tell(hello, ahead)
        pl.when(not_first == 1)(lambda: tell(ready, behind))

    def release(sem):
        pl.when(odd == 1)(lambda: tell(sem, behind))

    def begin(h):
        for d in range(3):
            for kv in range(2):
                y_copy(h, kv, d).start()

    def begin_x(h):
        for kv in range(2):
            loads[h * 2 + kv].wait()
            for side in range(2):
                x_copy(h, kv, y, side).start()

    def spread(h):
        for yy in near:
            for kv in range(2):
                wait_y(h, kv, yy)
                for side in range(2):
                    x_copy(h, kv, yy, side).start()

    order = (y, *near)

    def pass_on(h, i):
        yy = order[i]
        wait_x(h, 0, yy, 0)
        relay_copy(h, 0, yy).start()
        wait_x(h, 1, yy, 1)
        relay_copy(h, 1, yy).start()

    def work(h, i):
        if i == 0:
            first(h)
            chunk(h, x)
        if i == 1:
            for yy in order:
                wait_x(h, 1, yy, 0)
            chunk(h, lax.rem(x + 3, SIDE))
        if i == 2:
            for yy in order:
                wait_x(h, 0, yy, 1)
            chunk(h, lax.rem(x + 1, SIDE))
        if i == 3:
            for yy in order:
                for kv in range(2):
                    wait_relay(h, kv, yy)
            if h == 0:
                pl.when((odd == 1) & (not_last == 1))(lambda: pl.semaphore_wait(ready, 1))
            for slots in ((0,), (1, 2)):
                chunk(h, lax.rem(x + 2, SIDE), slots)
                finish(h, slots)

    for h in range(KVH):
        begin_x(h)
        pl.when(odd == 1)(functools.partial(begin, h))
    @pl.when(odd == 0)
    def _():
        pl.semaphore_wait(go_y, 1)
        for h in range(KVH):
            begin(h)
        pl.semaphore_wait(go, 1)

    for h in range(2):
        spread(h)
        if GY == h:
            release(go_y)
        if GX == h:
            release(go)
    loads[8].wait()
    loads[9].wait()
    loads[10].wait()
    for h in range(KVH):
        for i in range(SIDE):
            pass_on(h, i)
            if 0 < h < KVH - 1 or h > 0 and i < 2:
                work(h - 1, i)
        if GX == h + 4:
            release(go)
        if h + 2 < KVH:
            spread(h + 2)
            if GY == h + 2:
                pl.when(odd == 1)(lambda: pl.semaphore_wait(hello, 1))
                release(go_y)
    work(KVH - 2, 2)
    work(KVH - 2, 3)
    for i in range(SIDE):
        work(KVH - 1, i)

    if via:
        @pl.when(is_via)
        def _():
            for h in range(VIA):
                transit_copy(h).wait_recv()
                landing_copy(h).start()

    slot = lax.broadcasted_iota(jnp.int32, (1, 3), 1)
    totals = [jnp.sum(sums[i], axis=-1, keepdims=True) for i in range(3)]
    place = slot - (slot > move).astype(jnp.int32)
    kept_score = jnp.where(place <= 0, totals[1], totals[2])
    score_ref[...] = jnp.where(
        slot == move, totals[0], jnp.where(slot < count, kept_score, 0.0))

    for h in range(KVH):
        for kv in range(2):
            for d in range(3):
                y_copy(h, kv, d).wait_send()
            for yy in range(SIDE):
                for side in range(2):
                    x_copy(h, kv, yy, side).wait_send()
                relay_copy(h, kv, yy).wait_send()

    for h in range(KVH):
        guest_copy(h).wait_recv()
        for j in range(2):
            is_own = (kept > j).astype(jnp.bfloat16)
            is_guest = (kept == j).astype(jnp.bfloat16)
            c = h * 2 * HD
            att_ref[j, :, c:c + 2 * HD] = own[j, :, c:c + 2 * HD] * is_own + guest[h] * is_guest

    if via:
        @pl.when(is_via)
        def _():
            for h in range(VIA):
                landing_copy(h).wait_send()

    for h in range(KVH):
        guest_copy(h).wait_send()


def body(
    passage_query, passage_keyval, prefix_keys, prefix_values, home_count, move_slot, score_weight
):
    query = passage_query[0, 0]
    keyval = passage_keyval[0, 0]
    slots, tokens, width = query.shape
    rows = prefix_keys.shape[1]
    lanes = lax.axis_size("lane")
    any_ = pl.BlockSpec(memory_space=pl.ANY)
    smem = pl.BlockSpec(memory_space=pltpu.SMEM)
    vmem = pl.BlockSpec(memory_space=pltpu.VMEM)
    bf16, f32 = jnp.bfloat16, jnp.float32
    dma = pltpu.SemaphoreType.DMA
    attended, scores = pl.pallas_call(
        kernel,
        out_shape=(
            pltpu.VMEM((2, tokens, width), bf16),
            pltpu.VMEM((1, slots), f32),
        ),
        in_specs=[any_, any_, any_, any_, smem, smem, any_],
        out_specs=(vmem, vmem),
        scratch_shapes=[
            pltpu.VMEM((KVH, rows * lanes, HD), bf16),
            pltpu.VMEM((KVH, rows * lanes, HD), bf16),
            pltpu.VMEM(query.shape, bf16),
            pltpu.VMEM(keyval.shape, bf16),
            pltpu.VMEM((3, 2 * tokens, HD), f32),
            pltpu.VMEM((3, 2 * tokens, tokens), f32),
            pltpu.VMEM((2, tokens, width), bf16),
            pltpu.VMEM((KVH, tokens, 2 * HD), bf16),
            pltpu.VMEM((KVH, tokens, 2 * HD), bf16),
            pltpu.VMEM((VIA, tokens, 2 * HD), bf16),
            pltpu.VMEM((3, 1, HD), f32),
            pltpu.VMEM(score_weight.shape, bf16),
            dma((11,)),
            dma((KVH, 2, 3)),
            dma((KVH, 2, SIDE, 2)),
            dma((KVH, 2, SIDE)),
            dma((KVH, 2, SIDE)),
            dma((KVH, 2, SIDE, 2)),
            dma((KVH, 2, SIDE)),
            dma((KVH,)),
            dma((KVH,)),
            dma((VIA,)),
            dma((VIA,)),
            pltpu.SemaphoreType.REGULAR,
            pltpu.SemaphoreType.REGULAR,
            pltpu.SemaphoreType.REGULAR,
            pltpu.SemaphoreType.REGULAR,
        ],
        compiler_params=pltpu.CompilerParams(
            collective_id=0, has_side_effects=True, vmem_limit_bytes=60 * 2**20),
    )(query, keyval, prefix_keys[0], prefix_values[0], home_count, move_slot, score_weight)
    return attended[None, None], scores[None]


def solution(mesh):
    in_specs = (
        P("grp", "lane", None, None, None),
        P("grp", "lane", None, None, None, None),
        P("grp", "lane", None),
        P("grp", "lane", None),
        P("grp", "lane"),
        P("grp", "lane"),
        P(),
    )
    out_specs = (P("grp", "lane", None, None, None), P("grp", "lane", None))
    return jax.shard_map(body, mesh=mesh, in_specs=in_specs, out_specs=out_specs, check_vma=False)
```
